32 devices in a mesh: replica: 4 (over z), fsdp: 8 (over y, x, core).
Axes of the slice: x: 2, y: 2, z: 4, core: 2. Of those that a mesh axis runs over, the one named last changes fastest.
Arguments:
- frames: bfloat16 [2, 8192, 3072], P(None, ('replica', 'fsdp')), may hold values from -0.3984375 to 0.3984375
- out_weight: bfloat16 [3072, 2048], P('fsdp'), may hold values from -200 to 200
- align: int32 [2, 8192], P(None, ('replica', 'fsdp')), may hold values from 0 to 2047
- lengths: int32 [2, 32], P(None, ('replica', 'fsdp')), may hold values from 64 to 256, as said below
- deltas: float32 [16, 4, 524288], P(None, 'replica', 'fsdp'), may hold values from -6 to 6
- momentum: float32 [16, 524288], P(None, 'fsdp'), may hold values from -6 to 6
- fragment: int32 [1], replicated, may hold values from 0 to 15
Outputs:
- weight_grad: bfloat16 [4, 3072, 2048], P('replica', 'fsdp')
- frame_grad: bfloat16 [2, 8192, 3072], P(None, ('replica', 'fsdp'))
- loss: float32 [4], P('replica')
- new_momentum: float32 [524288], P('fsdp')
- outer_step: float32 [524288], P('fsdp')
The draws below stay inside these ranges and needn't reach their ends.
Inputs may be any that keep to these rules, and one draw needn't show every extreme that they name: `lengths`: one slot of every micro-batch holds a full utterance of 256 frames.
All inputs are finite; a program needn't handle non-finite values.
Results may differ from the reference program's by a relative error of at most 0.017.
The reference program's roundings to bfloat16 on the way count: a program that leaves them out, or rounds other values in their place, can miss the bound.
Values may be sent and summed in bfloat16 or wider, within the bound.
A program may use at most 128 MiB of HBM per device.

```python
import jax
import jax.numpy as jnp
from jax import lax

D = 3072
S = 2048
MB = 2
TOK_DEV = 256
NFRAG = 16
SEQS = 32
ROWS = 8192
FRAG = 524288
N_REPLICA = 4
N_FSDP = 8


def draw_lengths(key, part):
    drawn = jax.random.randint(key, (MB, SEQS), TOK_DEV // 4, TOK_DEV + 1)
    column = jnp.arange(SEQS, dtype=jnp.int32)[None, :]
    return jnp.where(column == 0, TOK_DEV, drawn).astype(jnp.int32)


def draw_out_weight(key, part):
    base = jax.random.normal(jax.random.fold_in(key, 1), (D, S), jnp.float32) * D ** (-0.5)
    return base.astype(jnp.bfloat16)


def place_ends(values, own_key, low, high):
    place = [jax.random.randint(jax.random.fold_in(own_key, axis), (), 0, length) for axis, length in enumerate(values.shape)]
    main_axis = values.shape.index(max(values.shape))
    beside = place[:main_axis] + [(place[main_axis] + 1) % values.shape[main_axis]] + place[main_axis + 1:]
    return values.at[tuple(place)].set(low).at[tuple(beside)].set(high)


def levels(key, extent, shards, least, high):
    def one(dim, blocks):
        steps = jax.random.uniform(jax.random.fold_in(jax.random.fold_in(key, 6), dim), (blocks,), jnp.float32, least / len(shards), high / len(shards))
        return jnp.repeat(jnp.exp(steps), extent[dim] // blocks).reshape((-1,) + (1,) * (len(extent) - dim - 1))

    gain = one(*shards[0])
    for cut in shards[1:]:
        gain = gain * one(*cut)
    return gain


def noise(key, shape, spread, limit, pieces=(), held_as=jnp.bfloat16):
    values = jax.random.normal(key, shape, jnp.float32) * spread
    if len(pieces) > 0:
        values = levels(key, shape, pieces, -0.22, 0.18) * values
    return jnp.clip(values, min=-limit, max=limit).astype(held_as)


def setup_inputs(seed: int = 0) -> dict:
    keys = jax.random.split(jax.random.key(seed), 8)
    return {
        "frames": noise(keys[0], (MB, ROWS, D), 0.05, 0.3984375, ((1, 32),)),
        "out_weight": draw_out_weight(jax.random.fold_in(keys[7], 71), 0),
        "align": place_ends(jax.random.randint(keys[2], (MB, ROWS), 0, S), jax.random.fold_in(keys[2], 1), 0, S - 1).astype(jnp.int32),
        "lengths": draw_lengths(jax.random.fold_in(keys[7], 71), 0),
        "deltas": noise(keys[4], (NFRAG, N_REPLICA, FRAG), 1.0, 6.0, ((1, 4), (2, 8)), jnp.float32),
        "momentum": noise(keys[5], (NFRAG, FRAG), 1.0, 6.0, ((1, 8),), jnp.float32),
        "fragment": jax.random.randint(keys[6], (1,), 0, NFRAG).astype(jnp.int32),
    }


def reference(frames, out_weight, align, lengths, deltas, momentum, fragment):
    group_rows = N_FSDP * TOK_DEV
    weight_parts = []
    grad_parts = []
    loss_parts = []
    for group in range(N_REPLICA):
        block = frames[:, group * group_rows:(group + 1) * group_rows, :].reshape(MB * group_rows, D).astype(jnp.float32)
        labels = align[:, group * group_rows:(group + 1) * group_rows].reshape(MB * group_rows)
        slot_len = lengths[:, group * N_FSDP:(group + 1) * N_FSDP]
        position = jnp.arange(TOK_DEV, dtype=jnp.int32)
        valid = (position[None, None, :] < slot_len[:, :, None]).astype(jnp.float32).reshape(MB * group_rows)
        center = block - lax.optimization_barrier(jnp.mean(block, axis=1, keepdims=True))
        inv_std = lax.rsqrt(lax.optimization_barrier(jnp.mean(center * center, axis=1, keepdims=True)) + 1e-05)
        normed = center * inv_std
        normed_b = normed.astype(jnp.bfloat16)
        logits = jnp.dot(normed_b, out_weight, preferred_element_type=jnp.float32)
        logp = jax.nn.log_softmax(logits, axis=1)
        onehot = (labels[:, None] == jnp.arange(S, dtype=jnp.int32)[None, :]).astype(jnp.float32)
        picked = lax.optimization_barrier(jnp.sum(onehot * logp, axis=1))
        loss_parts.append(-jnp.sum(valid * picked) / (MB * group_rows))
        dlogits = (valid[:, None] * (jnp.exp(logp) - onehot)).astype(jnp.bfloat16)
        normed_shards = normed_b.reshape(MB, N_FSDP, TOK_DEV, D)
        dlogit_shards = dlogits.reshape(MB, N_FSDP, TOK_DEV, S)
        total = jnp.zeros((D, S), jnp.float32)
        for shard in range(N_FSDP):
            left = normed_shards[:, shard].reshape(MB * TOK_DEV, D)
            right = dlogit_shards[:, shard].reshape(MB * TOK_DEV, S)
            term = jnp.dot(left.T, right, preferred_element_type=jnp.float32).astype(jnp.bfloat16)
            total = total + term.astype(jnp.float32)
        weight_parts.append(total.astype(jnp.bfloat16))
        dnormed = jnp.dot(dlogits, out_weight.T, preferred_element_type=jnp.float32)
        mean_grad = lax.optimization_barrier(jnp.mean(dnormed, axis=1, keepdims=True))
        mean_proj = lax.optimization_barrier(jnp.mean(dnormed * normed, axis=1, keepdims=True))
        grad_rows = (inv_std * (dnormed - mean_grad - normed * mean_proj)).astype(jnp.bfloat16)
        grad_parts.append(grad_rows.reshape(MB, group_rows, D))
    weight_grad = jnp.stack(weight_parts, axis=0)
    frame_grad = jnp.concatenate(grad_parts, axis=1)
    loss = jnp.stack(loss_parts, axis=0)
    chosen = lax.dynamic_index_in_dim(deltas, fragment[0], 0, keepdims=False)
    average = lax.optimization_barrier(jnp.sum(chosen, axis=0)) / N_REPLICA
    previous = lax.dynamic_index_in_dim(momentum, fragment[0], 0, keepdims=False)
    new_momentum = 0.9 * previous + average
    outer_step = average + 0.9 * new_momentum
    return (weight_grad, frame_grad, loss, new_momentum, outer_step)
```

```python
import functools

import jax
import jax.numpy as jnp
from jax import lax
from jax.experimental import pallas as pl
from jax.experimental.pallas import tpu as pltpu
from jax.sharding import PartitionSpec as P

MESH = pl.DeviceIdType.MESH
F32 = jnp.float32
BF16 = jnp.bfloat16


def flip(index, mask):
    bit = 1
    out = index
    while bit <= mask:
        if mask & bit:
            out = out + bit * (1 - 2 * ((index // bit) % 2))
        bit *= 2
    return out


def popcount(value):
    return bin(value).count("1")


def plan(links):
    chips = 2**links
    ids = {}

    def new(key):
        ids[key] = len(ids)

    new(("own_core",))
    for p in range(links):
        for m in range(1, chips):
            new(("gather", p, m))
            new(("gather_core", p, m))
    for m in range(chips):
        new(("term_core", m))
    for p in range(links):
        for s in range(links):
            for m in range(chips):
                if all(not m & order(links, p)[t] for t in range(s + 1)):
                    new(("reduce", p, s, m))
    return ids


def order(links, p):
    return [1 << ((p + s) % links) for s in range(links)]


def kernel(n, groups, links, ids, slots, frames_hbm, w_hbm, lab_ref, mine_ref, prev_ref,
           wg_hbm, fg_hbm, loss_ref, mom_ref, step_ref,
           fbuf, inv_ref, nb, nbt, wbuf, logits, dl, dn, tb, crecv, rx, wgbuf,
           dsend, drecv, losssend, lossrecv,
           send, recv, small_send, small_recv, local):
    me = lax.axis_index("fsdp")
    group = lax.axis_index("replica")
    core = me % 2
    other = 1 - core
    chip = me // 2
    chips = 2**links
    rows, width = fbuf.shape
    depth, states = w_hbm.shape
    part = depth // links
    both = 2 * depth
    ntile = 256

    def peer(bit):
        return {"fsdp": flip(me, 2 * bit)}

    sibling = {"fsdp": flip(me, 1)}

    def rdma(key, src, dst, where):
        i = ids[key]
        return pltpu.make_async_remote_copy(
            src_ref=src, dst_ref=dst, send_sem=send.at[i], recv_sem=recv.at[i],
            device_id=where, device_id_type=MESH)

    frames_in = pltpu.make_async_copy(frames_hbm, fbuf, local.at[0])
    frames_in.start()
    own_in = pltpu.make_async_copy(w_hbm, wbuf.at[0, core], local.at[1])
    own_in.start()

    barrier = pltpu.get_barrier_semaphore()
    for k in range(1, n):
        pl.semaphore_signal(barrier, inc=1, device_id={"fsdp": flip(me, k)}, device_id_type=MESH)
    for k in range(1, groups):
        pl.semaphore_signal(
            barrier, inc=1, device_id={"replica": lax.rem(group + k, groups)}, device_id_type=MESH)
    pl.semaphore_wait(barrier, n - 1 + groups - 1)

    started = []

    def go(copy):
        copy.start()
        started.append(copy)

    def span(p):
        return pl.ds(p * part, part)

    def gather_copy(p, s, m):
        bit = order(links, p)[s]
        src = w_hbm.at[span(p)] if m == 0 else wbuf.at[m, core, span(p)]
        return rdma(("gather", p, m | bit), src, wbuf.at[m | bit, core, span(p)], peer(bit))

    def gather_core_copy(p, m):
        return rdma(("gather_core", p, m), wbuf.at[m, core, span(p)],
                    wbuf.at[m, core, span(p)], sibling)

    for s in range(links):
        for p in range(links):
            go(gather_copy(p, s, 0))
    own_core = rdma(("own_core",), w_hbm, wbuf.at[0, core], sibling)
    go(own_core)

    dsend[...] = mine_ref[...].astype(BF16)
    small = []
    for k in range(1, groups):
        copy = pltpu.make_async_remote_copy(
            src_ref=dsend, dst_ref=drecv.at[k - 1], send_sem=small_send.at[k - 1],
            recv_sem=small_recv.at[k - 1],
            device_id={"replica": lax.rem(group + k, groups)}, device_id_type=MESH)
        copy.start()
        small.append(copy)

    frames_in.wait()

    tile = 16

    def norm_tile(i, carry):
        r = pl.ds(pl.multiple_of(i * tile, tile), tile)
        x = fbuf[r, :].astype(F32)
        center = x - jnp.mean(x, axis=1, keepdims=True)
        inv = lax.rsqrt(jnp.mean(center * center, axis=1, keepdims=True) + 1e-05)
        nb[r, :] = (center * inv).astype(BF16)
        inv_ref[r, :] = inv
        return carry

    lax.fori_loop(0, rows // tile, norm_tile, 0)

    def transpose_tile(i, carry):
        c = pl.ds(pl.multiple_of(i * ntile, ntile), ntile)
        nbt[c, :] = nb[:, c].T
        return carry

    def columns(m):
        return pl.ds(pl.multiple_of(flip(chip, m) * both, both), both)

    def logits_chip(m, first):
        lhs = nb[:, columns(m)]

        def body(i, carry):
            c = pl.ds(pl.multiple_of(i * ntile, ntile), ntile)
            w = wbuf[m, :, :, c].reshape(both, ntile)
            out = jnp.dot(lhs, w, preferred_element_type=F32)
            if first:
                logits[:, c] = out
            else:
                logits[:, c] += out
            return carry

        lax.fori_loop(0, states // ntile, body, 0)

    arrivals = []
    for m in range(1, chips):
        for p in range(links):
            bits = order(links, p)
            last = max(s for s in range(links) if m & bits[s])
            arrivals.append((popcount(m), last, p, m))
    arrivals.sort()

    def arrive(last, p, m):
        bits = order(links, p)
        gather_copy(p, last, m & ~bits[last]).wait_recv()
        for s in range(last + 1, links):
            go(gather_copy(p, s, m))
        go(gather_core_copy(p, m))

    done = set()
    logged = [False]

    def ready_dots():
        for m in range(1, chips):
            if m not in done and all((p, m) in seen for p in range(links)):
                done.add(m)
                for p in range(links):
                    gather_core_copy(p, m).wait_recv()
                logits_chip(m, False)

    seen = set()
    for index, (_, last, p, m) in enumerate(arrivals):
        arrive(last, p, m)
        seen.add((p, m))
        if index == links - 1:
            lax.fori_loop(0, width // ntile, transpose_tile, 0)
            own_in.wait()
            own_core.wait_recv()
            logits_chip(0, True)
        if index >= links - 1 and (index + 1) % links == 0:
            ready_dots()
    ready_dots()

    def softmax_tile(i, total):
        r = pl.ds(pl.multiple_of(i * tile, tile), tile)
        z = logits[r, :]
        lab = lab_ref[r, :]
        top = jnp.max(z, axis=1, keepdims=True)
        e = jnp.exp(z - top)
        norm = jnp.sum(e, axis=1, keepdims=True)
        valid = (lab >= 0).astype(F32)
        hit = lax.broadcasted_iota(jnp.int32, (tile, states), 1) == lab
        picked = jnp.sum(jnp.where(hit, z, 0.0), axis=1, keepdims=True)
        scale = valid / norm
        d = e * scale
        dl[r, :] = jnp.where(hit, d - 1.0, d).astype(BF16)
        return total + valid * (top + jnp.log(norm) - picked)

    total = lax.fori_loop(0, rows // tile, softmax_tile, jnp.zeros((tile, 1), F32))

    slot_of = slots

    def term(m):
        lhs = nbt[columns(m), :]

        def body(i, carry):
            c = pl.ds(pl.multiple_of(i * ntile, ntile), ntile)
            out = jnp.dot(lhs, dl[:, c], preferred_element_type=F32).astype(BF16)
            tb[m, :, :, c] = out.reshape(2, depth, ntile)
            return carry

        lax.fori_loop(0, states // ntile, body, 0)

    def term_copy(m):
        return rdma(("term_core", m), tb.at[m, other], crecv.at[m], sibling)

    def reduce_copy(p, s, m):
        bit = order(links, p)[s]
        there = m & ~bit
        return rdma(("reduce", p, s, there), tb.at[m, core, span(p)],
                    rx.at[slot_of[(p, s, there)]], peer(bit))

    add_tile = 32

    def add_core(m):
        def body(i, carry):
            r = pl.ds(pl.multiple_of(i * add_tile, add_tile), add_tile)
            tb[m, core, r, :] = (tb[m, core, r, :].astype(F32) + crecv[m, r, :].astype(F32)).astype(BF16)
            return carry

        lax.fori_loop(0, depth // add_tile, body, 0)

    def finish_core(m):
        term_copy(m).wait_recv()
        add_core(m)
        for p in range(links):
            if m & order(links, p)[0]:
                go(reduce_copy(p, 0, m))

    masks = sorted(range(chips), key=lambda m: (-popcount(m), m))
    for index, m in enumerate(masks):
        term(m)
        go(term_copy(m))
        if index:
            finish_core(masks[index - 1])
    finish_core(masks[-1])

    losssend[...] = jnp.broadcast_to(jnp.sum(total, axis=0, keepdims=True), losssend.shape)
    losses = []
    for k in range(1, n):
        copy = pltpu.make_async_remote_copy(
            src_ref=losssend, dst_ref=lossrecv.at[k - 1],
            send_sem=small_send.at[groups - 2 + k], recv_sem=small_recv.at[groups - 2 + k],
            device_id={"fsdp": flip(me, k)}, device_id_type=MESH)
        copy.start()
        losses.append(copy)

    def dnormed(m):
        w = wbuf[m].reshape(both, states)
        half = rows // 2

        def body(i, carry):
            r = pl.ds(pl.multiple_of(i * half, half), half)
            dn[r, columns(m)] = lax.dot_general(
                dl[r, :], w, (((1,), (1,)), ((), ())), preferred_element_type=F32)
            return carry

        lax.fori_loop(0, 2, body, 0)

    for m in masks:
        dnormed(m)

    def add_received(p, s, m):
        def body(i, carry):
            r = pl.multiple_of(i * add_tile, add_tile)
            here = pl.ds(p * part + r, add_tile)
            value = tb[m, core, here, :].astype(F32)
            for t in range(s):
                value = value + rx[slot_of[(p, t, m)], pl.ds(r, add_tile), :].astype(F32)
            if m == 0:
                wgbuf[here, :] = value.astype(BF16)
            else:
                tb[m, core, here, :] = value.astype(BF16)
            return carry

        lax.fori_loop(0, part // add_tile, body, 0)

    def reduce_wait(p, s, m):
        bit = order(links, p)[s]
        reduce_copy(p, s, m | bit).wait_recv()

    waited = set()

    def need(p, s, m):
        for t in range(s):
            if (p, t, m) not in waited:
                waited.add((p, t, m))
                reduce_wait(p, t, m)

    for s in range(1, links):
        for p in range(links):
            bits = order(links, p)
            for m in masks:
                if m & bits[s] and all(not m & bits[t] for t in range(s)):
                    need(p, s, m)
                    add_received(p, s, m)
                    go(reduce_copy(p, s, m))

    def grad_tile(i, carry):
        r = pl.ds(pl.multiple_of(i * tile, tile), tile)
        d = dn[r, :]
        x = nb[r, :].astype(F32)
        mean_grad = jnp.mean(d, axis=1, keepdims=True)
        mean_proj = jnp.mean(d * x, axis=1, keepdims=True)
        fbuf[r, :] = (inv_ref[r, :] * (d - mean_grad - x * mean_proj)).astype(BF16)
        return carry

    lax.fori_loop(0, rows // tile, grad_tile, 0)
    frames_out = pltpu.make_async_copy(fbuf, fg_hbm, local.at[0])
    frames_out.start()

    for copy in small:
        copy.wait_recv()
    average = mine_ref[...].astype(BF16).astype(F32)
    for k in range(1, groups):
        average = average + drecv[k - 1].astype(F32)
    average = average * (1.0 / groups)
    momentum = 0.9 * prev_ref[...] + average
    mom_ref[...] = momentum
    step_ref[...] = average + 0.9 * momentum

    for copy in losses:
        copy.wait_recv()
    value = losssend[...]
    for k in range(1, n):
        value = value + lossrecv[k - 1]
    loss_ref[...] = value * (1.0 / (rows * n))

    for p in range(links):
        need(p, links, 0)
        add_received(p, links, 0)
    grad_out = pltpu.make_async_copy(wgbuf, wg_hbm, local.at[1])
    grad_out.start()
    for copy in started + small + losses:
        copy.wait_send()
    frames_out.wait()
    grad_out.wait()


def per_device(frames, out_weight, align, lengths, deltas, momentum, fragment):
    n = lax.axis_size("fsdp")
    groups = lax.axis_size("replica")
    links = n.bit_length() - 2
    chips = 2**links
    micro, per, width = frames.shape
    rows = micro * per
    depth, states = out_weight.shape
    part = depth // links
    chosen = lax.dynamic_index_in_dim(deltas, fragment[0], 0, keepdims=False)[0]
    previous = lax.dynamic_index_in_dim(momentum, fragment[0], 0, keepdims=False)
    entries = chosen.shape[0]
    lanes = (entries // 128, 128)
    position = jnp.arange(per, dtype=jnp.int32)
    lab = jnp.where(position[None, :] < lengths, align, -1).reshape(rows, 1)

    ids = plan(links)
    slots = {}
    for key in ids:
        if key[0] == "reduce":
            slots[key[1:]] = len(slots)
    nsmall = groups - 1 + n - 1
    hbm = pl.BlockSpec(memory_space=pl.ANY)
    vmem = pl.BlockSpec(memory_space=pltpu.VMEM)
    flops = 6 * rows * width * states
    wg, fg, loss, mom, step = pl.pallas_call(
        functools.partial(kernel, n, groups, links, ids, slots),
        out_shape=(
            jax.ShapeDtypeStruct((depth, states), BF16),
            jax.ShapeDtypeStruct((rows, width), BF16),
            jax.ShapeDtypeStruct((8, 128), F32),
            jax.ShapeDtypeStruct(lanes, F32),
            jax.ShapeDtypeStruct(lanes, F32),
        ),
        in_specs=[hbm, hbm, vmem, vmem, vmem],
        out_specs=[hbm, hbm, vmem, vmem, vmem],
        scratch_shapes=[
            pltpu.VMEM((rows, width), BF16),
            pltpu.VMEM((rows, 1), F32),
            pltpu.VMEM((rows, width), BF16),
            pltpu.VMEM((width, rows), BF16),
            pltpu.VMEM((chips, 2, depth, states), BF16),
            pltpu.VMEM((rows, states), F32),
            pltpu.VMEM((rows, states), BF16),
            pltpu.VMEM((rows, width), F32),
            pltpu.VMEM((chips, 2, depth, states), BF16),
            pltpu.VMEM((chips, depth, states), BF16),
            pltpu.VMEM((len(slots), part, states), BF16),
            pltpu.VMEM((depth, states), BF16),
            pltpu.VMEM(lanes, BF16),
            pltpu.VMEM((groups - 1,) + lanes, BF16),
            pltpu.VMEM((8, 128), F32),
            pltpu.VMEM((n - 1, 8, 128), F32),
            pltpu.SemaphoreType.DMA((len(ids),)),
            pltpu.SemaphoreType.DMA((len(ids),)),
            pltpu.SemaphoreType.DMA((nsmall,)),
            pltpu.SemaphoreType.DMA((nsmall,)),
            pltpu.SemaphoreType.DMA((2,)),
        ],
        compiler_params=pltpu.CompilerParams(
            collective_id=0, has_side_effects=True, vmem_limit_bytes=63 * 2**20),
        cost_estimate=pl.CostEstimate(
            flops=flops, bytes_accessed=4 * rows * width, transcendentals=rows * states),
    )(frames.reshape(rows, width), out_weight, lab, chosen.reshape(lanes), previous.reshape(lanes))
    return (
        wg.reshape(1, depth, states),
        fg.reshape(micro, per, width),
        loss[0, :1],
        mom.reshape(entries),
        step.reshape(entries),
    )


def solution(mesh):
    return jax.shard_map(
        per_device,
        mesh=mesh,
        in_specs=(
            P(None, ("replica", "fsdp"), None),
            P("fsdp", None),
            P(None, ("replica", "fsdp")),
            P(None, ("replica", "fsdp")),
            P(None, "replica", "fsdp"),
            P(None, "fsdp"),
            P(),
        ),
        out_specs=(
            P("replica", "fsdp", None),
            P(None, ("replica", "fsdp"), None),
            P("replica"),
            P("fsdp"),
            P("fsdp"),
        ),
        check_vma=False,
    )
```

```python
import functools

import jax
import jax.numpy as jnp
from jax import lax
from jax.experimental import pallas as pl
from jax.experimental.pallas import tpu as pltpu
from jax.sharding import PartitionSpec as P

MESH = pl.DeviceIdType.MESH
F32 = jnp.float32
BF16 = jnp.bfloat16


def flip(index, mask):
    bit = 1
    out = index
    while bit <= mask:
        if mask & bit:
            out = out + bit * (1 - 2 * ((index // bit) % 2))
        bit *= 2
    return out


def popcount(value):
    return bin(value).count("1")


def pieces(depth, links):
    subs = links if depth % (48 * links) == 0 else 1
    size = depth // (3 * subs)
    return [(third, i, (third + i) % links if subs == 1 else i, size) for third in range(3) for i in range(subs)]


def plan(links, depth):
    chips = 2**links
    ids = {}

    def new(key):
        ids[key] = len(ids)

    new(("own_core",))
    for g in range(len(pieces(depth, links))):
        for m in range(1, chips):
            new(("gather", g, m))
            new(("gather_core", g, m))
    for m in range(chips):
        new(("term_core", m))
    for p in range(links):
        for s in range(links):
            for m in range(chips):
                if all(not m & order(links, p)[t] for t in range(s + 1)):
                    new(("reduce", p, s, m))
    return ids


def order(links, p):
    return [1 << ((p + s) % links) for s in range(links)]


def kernel(n, groups, links, ids, slots, frames_hbm, w_hbm, lab_ref, mine_ref, prev_ref,
           wg_hbm, fg_hbm, loss_ref, mom_ref, step_ref,
           fbuf, inv_ref, nb, nbt, wbuf, logits, dl, dn, tb, crecv, rx,
           dsend, drecv, losssend, lossrecv,
           send, recv, small_send, small_recv, local):
    me = lax.axis_index("fsdp")
    group = lax.axis_index("replica")
    core = me % 2
    other = 1 - core
    chip = me // 2
    chips = 2**links
    rows, width = fbuf.shape
    depth, states = w_hbm.shape
    part = depth // links
    both = 2 * depth
    ntile = 256

    def peer(bit):
        return {"fsdp": flip(me, 2 * bit)}

    sibling = {"fsdp": flip(me, 1)}

    def rdma(key, src, dst, where):
        i = ids[key]
        return pltpu.make_async_remote_copy(
            src_ref=src, dst_ref=dst, send_sem=send.at[i], recv_sem=recv.at[i],
            device_id=where, device_id_type=MESH)

    frames_in = pltpu.make_async_copy(frames_hbm, fbuf, local.at[0])
    frames_in.start()
    own_in = pltpu.make_async_copy(w_hbm, wbuf.at[0, core], local.at[1])
    own_in.start()

    barrier = pltpu.get_barrier_semaphore()
    for k in range(1, n):
        pl.semaphore_signal(barrier, inc=1, device_id={"fsdp": flip(me, k)}, device_id_type=MESH)
    for k in range(1, groups):
        pl.semaphore_signal(
            barrier, inc=1, device_id={"replica": lax.rem(group + k, groups)}, device_id_type=MESH)
    pl.semaphore_wait(barrier, n - 1 + groups - 1)

    started = []

    def go(copy):
        copy.start()
        started.append(copy)

    def span(p):
        return pl.ds(p * part, part)

    cuts = pieces(depth, links)
    subs = len(cuts) // 3
    parity = group % 2
    partner = {"replica": flip(group, 1)}

    def cut(g):
        third, i, _, size = cuts[g]
        place = third + parity * (2 - 2 * third)
        return pl.ds(pl.multiple_of((place * subs + i) * size, size), size)

    def gather_copy(g, s, m):
        bit = order(links, cuts[g][2])[s]
        src = w_hbm.at[cut(g)] if m == 0 else wbuf.at[m, core, cut(g)]
        return rdma(("gather", g, m | bit), src, wbuf.at[m | bit, core, cut(g)], peer(bit))

    def gather_core_copy(g, m):
        return rdma(("gather_core", g, m), wbuf.at[m, core, cut(g)],
                    wbuf.at[m, core, cut(g)], sibling)

    def partner_copy(g, m):
        return rdma(("gather", g + 2 * subs, m), wbuf.at[m, core, cut(g)],
                    wbuf.at[m, core, cut(g)], partner)

    for third in range(2):
        for s in range(links):
            for g in range(third * subs, (third + 1) * subs):
                go(gather_copy(g, s, 0))
    own_core = rdma(("own_core",), w_hbm, wbuf.at[0, core], sibling)
    go(own_core)

    dsend[...] = mine_ref[...].astype(BF16)
    small = []
    for k in range(1, groups):
        copy = pltpu.make_async_remote_copy(
            src_ref=dsend, dst_ref=drecv.at[k - 1], send_sem=small_send.at[k - 1],
            recv_sem=small_recv.at[k - 1],
            device_id={"replica": lax.rem(group + k, groups)}, device_id_type=MESH)
        copy.start()
        small.append(copy)

    frames_in.wait()

    tile = 16

    def norm_tile(i, carry):
        r = pl.ds(pl.multiple_of(i * tile, tile), tile)
        x = fbuf[r, :].astype(F32)
        center = x - jnp.mean(x, axis=1, keepdims=True)
        inv = lax.rsqrt(jnp.mean(center * center, axis=1, keepdims=True) + 1e-05)
        nb[r, :] = (center * inv).astype(BF16)
        inv_ref[r, :] = inv
        return carry

    lax.fori_loop(0, rows // tile, norm_tile, 0, unroll=2)

    def transpose_tile(i, carry):
        c = pl.ds(pl.multiple_of(i * ntile, ntile), ntile)
        nbt[c, :] = nb[:, c].T
        return carry

    def columns(m):
        return pl.ds(pl.multiple_of(flip(chip, m) * both, both), both)

    def logits_chip(m, first):
        lhs = nb[:, columns(m)]

        def body(i, carry):
            c = pl.ds(pl.multiple_of(i * ntile, ntile), ntile)
            w = wbuf[m, :, :, c].reshape(both, ntile)
            out = jnp.dot(lhs, w, preferred_element_type=F32)
            if first:
                logits[:, c] = out
            else:
                logits[:, c] += out
            return carry

        lax.fori_loop(0, states // ntile, body, 0, unroll=2)

    arrivals = []
    ranks = sorted({(popcount(m), max(s for s in range(links) if m & order(links, 0)[s])) for m in range(1, chips)})
    for g, (third, _, path, _) in enumerate(cuts):
        bits = order(links, path)
        for m in range(1, chips):
            last = max(s for s in range(links) if m & bits[s])
            rank = ranks.index((popcount(m), last))
            arrivals.append((rank + (0, len(ranks), len(ranks) + 0.5)[third], g, last, m))
    arrivals.sort()

    def arrive(g, last, m):
        third, _, path, _ = cuts[g]
        bits = order(links, path)
        if third == 2:
            partner_copy(g - 2 * subs, m).wait_recv()
        else:
            gather_copy(g, last, m & ~bits[last]).wait_recv()
            for s in range(last + 1, links):
                go(gather_copy(g, s, m))
        if third == 0:
            go(partner_copy(g, m))
        go(gather_core_copy(g, m))

    done = set()
    seen = set()
    for index, (_, g, last, m) in enumerate(arrivals):
        arrive(g, last, m)
        seen.add((g, m))
        if index == subs - 1:
            lax.fori_loop(0, width // ntile, transpose_tile, 0)
        if index == 2 * subs - 1:
            own_in.wait()
            own_core.wait_recv()
            logits_chip(0, True)
        if index + 1 == len(arrivals) or arrivals[index + 1][0] != arrivals[index][0]:
            for m in range(1, chips):
                if m not in done and all((g, m) in seen for g in range(len(cuts))):
                    done.add(m)
                    for g in range(len(cuts)):
                        gather_core_copy(g, m).wait_recv()
                    logits_chip(m, False)

    def softmax_tile(i, total):
        r = pl.ds(pl.multiple_of(i * tile, tile), tile)
        z = logits[r, :]
        lab = lab_ref[r, :]
        top = jnp.max(z, axis=1, keepdims=True)
        e = jnp.exp(z - top)
        norm = jnp.sum(e, axis=1, keepdims=True)
        valid = (lab >= 0).astype(F32)
        hit = lax.broadcasted_iota(jnp.int32, (tile, states), 1) == lab
        picked = jnp.sum(jnp.where(hit, z, 0.0), axis=1, keepdims=True)
        scale = valid / norm
        d = e * scale
        dl[r, :] = jnp.where(hit, d - 1.0, d).astype(BF16)
        return total + valid * (top + jnp.log(norm) - picked)

    total = lax.fori_loop(0, rows // tile, softmax_tile, jnp.zeros((tile, 1), F32), unroll=2)

    slot_of = slots

    def term(m):
        lhs = nbt[columns(m), :]

        def body(i, carry):
            c = pl.ds(pl.multiple_of(i * ntile, ntile), ntile)
            out = jnp.dot(lhs, dl[:, c], preferred_element_type=F32).astype(BF16)
            tb[m, :, :, c] = out.reshape(2, depth, ntile)
            return carry

        lax.fori_loop(0, states // ntile, body, 0, unroll=2)

    def term_copy(m):
        return rdma(("term_core", m), tb.at[m, other], crecv.at[m], sibling)

    def reduce_copy(p, s, m):
        bit = order(links, p)[s]
        there = m & ~bit
        return rdma(("reduce", p, s, there), tb.at[m, core, span(p)],
                    rx.at[slot_of[(p, s, there)]], peer(bit))

    add_tile = 32

    def add_core(m):
        def body(i, carry):
            r = pl.ds(pl.multiple_of(i * add_tile, add_tile), add_tile)
            tb[m, core, r, :] = (tb[m, core, r, :].astype(F32) + crecv[m, r, :].astype(F32)).astype(BF16)
            return carry

        lax.fori_loop(0, depth // add_tile, body, 0, unroll=2)

    def finish_core(m):
        term_copy(m).wait_recv()
        add_core(m)
        for p in range(links):
            if m & order(links, p)[0]:
                go(reduce_copy(p, 0, m))

    masks = sorted(range(chips), key=lambda m: (-popcount(m), m))
    for index, m in enumerate(masks):
        term(m)
        go(term_copy(m))
        if index:
            finish_core(masks[index - 1])
    finish_core(masks[-1])

    losssend[...] = jnp.broadcast_to(jnp.sum(total, axis=0, keepdims=True), losssend.shape)
    losses = []
    for k in range(1, n):
        copy = pltpu.make_async_remote_copy(
            src_ref=losssend, dst_ref=lossrecv.at[k - 1],
            send_sem=small_send.at[groups - 2 + k], recv_sem=small_recv.at[groups - 2 + k],
            device_id={"fsdp": flip(me, k)}, device_id_type=MESH)
        copy.start()
        losses.append(copy)

    def dnormed(m):
        w = wbuf[m].reshape(both, states)
        half = rows // 2

        def body(i, carry):
            r = pl.ds(pl.multiple_of(i * half, half), half)
            dn[r, columns(m)] = lax.dot_general(
                dl[r, :], w, (((1,), (1,)), ((), ())), preferred_element_type=F32)
            return carry

        lax.fori_loop(0, 2, body, 0)

    for m in masks:
        dnormed(m)

    def add_received(p, s, m):
        def body(i, carry):
            r = pl.multiple_of(i * add_tile, add_tile)
            here = pl.ds(p * part + r, add_tile)
            value = tb[m, core, here, :].astype(F32)
            for t in range(s):
                value = value + rx[slot_of[(p, t, m)], pl.ds(r, add_tile), :].astype(F32)
            tb[m, core, here, :] = value.astype(BF16)
            return carry

        lax.fori_loop(0, part // add_tile, body, 0, unroll=2)

    def reduce_wait(p, s, m):
        bit = order(links, p)[s]
        reduce_copy(p, s, m | bit).wait_recv()

    waited = set()

    def need(p, s, m):
        for t in range(s):
            if (p, t, m) not in waited:
                waited.add((p, t, m))
                reduce_wait(p, t, m)

    for s in range(1, links):
        for p in range(links):
            bits = order(links, p)
            for m in masks:
                if m & bits[s] and all(not m & bits[t] for t in range(s)):
                    need(p, s, m)
                    add_received(p, s, m)
                    go(reduce_copy(p, s, m))

    def grad_tile(i, carry):
        r = pl.ds(pl.multiple_of(i * tile, tile), tile)
        d = dn[r, :]
        x = nb[r, :].astype(F32)
        mean_grad = jnp.mean(d, axis=1, keepdims=True)
        mean_proj = jnp.mean(d * x, axis=1, keepdims=True)
        fbuf[r, :] = (inv_ref[r, :] * (d - mean_grad - x * mean_proj)).astype(BF16)
        return carry

    lax.fori_loop(0, rows // tile, grad_tile, 0, unroll=2)
    frames_out = pltpu.make_async_copy(fbuf, fg_hbm, local.at[0])
    frames_out.start()

    for copy in small:
        copy.wait_recv()
    average = mine_ref[...].astype(BF16).astype(F32)
    for k in range(1, groups):
        average = average + drecv[k - 1].astype(F32)
    average = average * (1.0 / groups)
    momentum = 0.9 * prev_ref[...] + average
    mom_ref[...] = momentum
    step_ref[...] = average + 0.9 * momentum

    for copy in losses:
        copy.wait_recv()
    value = losssend[...]
    for k in range(1, n):
        value = value + lossrecv[k - 1]
    loss_ref[...] = value * (1.0 / (rows * n))

    for p in range(links):
        need(p, links, 0)
        add_received(p, links, 0)
    grad_out = pltpu.make_async_copy(tb.at[0, core], wg_hbm, local.at[1])
    grad_out.start()
    for copy in started + small + losses:
        copy.wait_send()
    frames_out.wait()
    grad_out.wait()


def per_device(frames, out_weight, align, lengths, deltas, momentum, fragment):
    n = lax.axis_size("fsdp")
    groups = lax.axis_size("replica")
    links = n.bit_length() - 2
    chips = 2**links
    micro, per, width = frames.shape
    rows = micro * per
    depth, states = out_weight.shape
    part = depth // links
    chosen = lax.dynamic_index_in_dim(deltas, fragment[0], 0, keepdims=False)[0]
    previous = lax.dynamic_index_in_dim(momentum, fragment[0], 0, keepdims=False)
    entries = chosen.shape[0]
    lanes = (entries // 128, 128)
    position = jnp.arange(per, dtype=jnp.int32)
    lab = jnp.where(position[None, :] < lengths, align, -1).reshape(rows, 1)

    ids = plan(links, depth)
    slots = {}
    for key in ids:
        if key[0] == "reduce":
            slots[key[1:]] = len(slots)
    nsmall = groups - 1 + n - 1
    hbm = pl.BlockSpec(memory_space=pl.ANY)
    vmem = pl.BlockSpec(memory_space=pltpu.VMEM)
    flops = 6 * rows * width * states
    wg, fg, loss, mom, step = pl.pallas_call(
        functools.partial(kernel, n, groups, links, ids, slots),
        out_shape=(
            jax.ShapeDtypeStruct((depth, states), BF16),
            jax.ShapeDtypeStruct((rows, width), BF16),
            jax.ShapeDtypeStruct((8, 128), F32),
            jax.ShapeDtypeStruct(lanes, F32),
            jax.ShapeDtypeStruct(lanes, F32),
        ),
        in_specs=[hbm, hbm, vmem, vmem, vmem],
        out_specs=[hbm, hbm, vmem, vmem, vmem],
        scratch_shapes=[
            pltpu.VMEM((rows, width), BF16),
            pltpu.VMEM((rows, 1), F32),
            pltpu.VMEM((rows, width), BF16),
            pltpu.VMEM((width, rows), BF16),
            pltpu.VMEM((chips, 2, depth, states), BF16),
            pltpu.VMEM((rows, states), F32),
            pltpu.VMEM((rows, states), BF16),
            pltpu.VMEM((rows, width), F32),
            pltpu.VMEM((chips, 2, depth, states), BF16),
            pltpu.VMEM((chips, depth, states), BF16),
            pltpu.VMEM((len(slots), part, states), BF16),
            pltpu.VMEM(lanes, BF16),
            pltpu.VMEM((groups - 1,) + lanes, BF16),
            pltpu.VMEM((8, 128), F32),
            pltpu.VMEM((n - 1, 8, 128), F32),
            pltpu.SemaphoreType.DMA((len(ids),)),
            pltpu.SemaphoreType.DMA((len(ids),)),
            pltpu.SemaphoreType.DMA((nsmall,)),
            pltpu.SemaphoreType.DMA((nsmall,)),
            pltpu.SemaphoreType.DMA((2,)),
        ],
        compiler_params=pltpu.CompilerParams(
            collective_id=0, has_side_effects=True, vmem_limit_bytes=63 * 2**20),
        cost_estimate=pl.CostEstimate(
            flops=flops, bytes_accessed=4 * rows * width, transcendentals=rows * states),
    )(frames.reshape(rows, width), out_weight, lab, chosen.reshape(lanes), previous.reshape(lanes))
    return (
        wg.reshape(1, depth, states),
        fg.reshape(micro, per, width),
        loss[0, :1],
        mom.reshape(entries),
        step.reshape(entries),
    )


def solution(mesh):
    return jax.shard_map(
        per_device,
        mesh=mesh,
        in_specs=(
            P(None, ("replica", "fsdp"), None),
            P("fsdp", None),
            P(None, ("replica", "fsdp")),
            P(None, ("replica", "fsdp")),
            P(None, "replica", "fsdp"),
            P(None, "fsdp"),
            P(),
        ),
        out_specs=(
            P("replica", "fsdp", None),
            P(None, ("replica", "fsdp"), None),
            P("replica"),
            P("fsdp"),
            P("fsdp"),
        ),
        check_vma=False,
    )
```
